256 devices in a mesh: rep: 8 (over z_lo, core), fsdp: 32 (over x, y, z_hi).
Axes of the slice: x: 4, y: 4, z: 8 (z_hi: 2, z_lo: 4; z = z_hi * 4 + z_lo), core: 2. Of those that a mesh axis runs over, the one named last changes fastest.
Arguments:
- inputs: bfloat16 [8, 12288, 8192], P('rep', 'fsdp'), may hold values from -12 to 12
- cotangent: bfloat16 [8, 12288, 512], P('rep', 'fsdp'), may hold values from -0.3125 to 0.3125
- weights: float32 [8, 8192, 512], P('rep', 'fsdp'), may hold values from -0.0625 to 0.0625
- first_moment: float32 [8, 8192, 512], P('rep', 'fsdp'), may hold values from -1.75 to 1.75
- second_moment: float32 [8, 8192, 512], P('rep', 'fsdp'), may hold values from 0.1 to 4
- pseudo_grad: float32 [8, 8192, 128], P('rep', 'fsdp'), may hold values from -6 to 6
- anchor: float32 [8192, 512], P('fsdp'), may hold values from -3 to 3
- momentum: float32 [8192, 512], P('fsdp'), may hold values from -6 to 6
- fragment: int32 [1], replicated, may hold values from 0 to 3
Outputs:
- projected: bfloat16 [8, 12288, 512], P('rep', 'fsdp')
- new_weights: float32 [8, 8192, 512], P('rep', 'fsdp')
- new_first: float32 [8, 8192, 512], P('rep', 'fsdp')
- new_second: float32 [8, 8192, 512], P('rep', 'fsdp')
- new_anchor: float32 [8192, 512], P('fsdp')
- new_momentum: float32 [8192, 512], P('fsdp')
The draws below stay inside these ranges and needn't reach their ends.
All inputs are finite; a program needn't handle non-finite values.
Results may differ from the reference program's by a relative error of at most 0.0049.
Values may be sent and summed in bfloat16 or wider, within the bound.
A program may use at most 128 MiB of HBM per device.

```python
import math
import jax
import jax.numpy as jnp
from jax import lax

D = 8192
K = 512
NFRAG = 4
FRAG_W = 128
TOKENS = 12288
REPS = 8
N_REP = 8


def spiked(result, own_key, source, target, shards_of, factor):
    def block_of(dim):
        return (jnp.arange(result.shape[dim]) // (result.shape[dim] // shards_of)).reshape((-1,) + (1,) * (result.ndim - 1 - dim))

    near = jax.random.permutation(own_key, shards_of)[block_of(target)]
    second = (block_of(target) + shards_of // 2) % shards_of
    return jnp.where((block_of(source) == near) | (block_of(source) == second), factor * result, result)


def block_levels(rng, dims, pieces, smallest, high):
    level, own = 1.0, jax.random.fold_in(rng, 6)
    for axis_at, blocks in pieces:
        heights = jnp.exp(jax.random.uniform(jax.random.fold_in(own, axis_at), (blocks,), jnp.float32, smallest / len(pieces), high / len(pieces)))
        level = level * jnp.repeat(heights, dims[axis_at] // blocks).reshape([-1 if axis == axis_at else 1 for axis in range(len(dims))])
    return level


def scatter_about(stream_key, extent, deviation, limit, pieces=(), dtype=jnp.bfloat16):
    array = deviation * jax.random.normal(stream_key, extent, jnp.float32)
    if pieces:
        array = array * block_levels(stream_key, extent, pieces, -0.22, 0.18)
    return jnp.clip(array, -limit, limit).astype(dtype)


def bell_draw_with(stream_key, extent, width, limit, pieces, heavy, dtype=jnp.bfloat16):
    drawn = width * jax.random.normal(stream_key, extent, jnp.float32)
    if pieces:
        drawn = drawn * block_levels(stream_key, extent, pieces, -0.22, 0.18)
    return jnp.clip(spiked(drawn, jax.random.fold_in(stream_key, 3), *heavy), -limit, limit).astype(dtype)


def setup_inputs(seed: int = 0) -> dict:
    key_list = jax.random.split(jax.random.key(seed), 10)
    inputs = bell_draw_with(key_list[0], (REPS, TOKENS, D), 1.0, 12.0, ((0, 8), (1, 32)), (1, 2, 32, 2.75))
    cotangent = scatter_about(key_list[1], (REPS, TOKENS, K), 0.05, 0.3125, ((0, 8), (1, 32)))
    weights = scatter_about(key_list[2], (REPS, D, K), D ** -0.5, 0.0625, ((0, 8), (1, 32)), jnp.float32)
    first_moment = scatter_about(key_list[3], (REPS, D, K), 0.3, 1.75, ((0, 8), (1, 32)), jnp.float32)
    second_moment = jnp.clip(jnp.exp(math.log(4.0) - 3.6888794 * jax.random.uniform(key_list[4], (REPS, D, K), jnp.float32) ** block_levels(key_list[4], (REPS, D, K), ((0, 8), (1, 32)), -0.2, 0.2)), 0.1, 4.0)
    pseudo_grad = scatter_about(key_list[5], (REPS, D, FRAG_W), 1.0, 6.0, ((0, 8), (1, 32)), jnp.float32)
    anchor = scatter_about(key_list[6], (D, K), 0.5, 3.0, ((0, 32),), jnp.float32)
    momentum = scatter_about(key_list[7], (D, K), 1.0, 6.0, ((0, 32),), jnp.float32)
    fragment = jax.random.randint(key_list[8], (1,), 0, NFRAG).astype(jnp.int32)
    return dict(inputs=inputs, cotangent=cotangent, weights=weights, first_moment=first_moment, second_moment=second_moment, pseudo_grad=pseudo_grad, anchor=anchor, momentum=momentum, fragment=fragment)


beta_one = 0.9
beta_two = 0.95
inner_rate = 0.002
weight_decay = 0.1
adam_epsilon = 1e-08
outer_rate = 0.7
outer_momentum = 0.9

def reference(inputs, cotangent, weights, first_moment, second_moment, pseudo_grad, anchor, momentum, fragment):
    frag_start = (fragment[0] * FRAG_W).astype(jnp.int32)
    zero_index = jnp.zeros((), jnp.int32)
    mean_delta = lax.optimization_barrier(jnp.sum(pseudo_grad, axis=0)) / N_REP
    mom_frag = lax.dynamic_slice_in_dim(momentum, frag_start, FRAG_W, 1)
    new_mom_frag = outer_momentum * mom_frag + mean_delta
    update = outer_rate * (outer_momentum * new_mom_frag + mean_delta)
    anchor_frag = lax.dynamic_slice_in_dim(anchor, frag_start, FRAG_W, 1)
    new_anchor = lax.dynamic_update_slice(anchor, anchor_frag - update, (zero_index, frag_start))
    new_momentum = lax.dynamic_update_slice(momentum, new_mom_frag, (zero_index, frag_start))
    keys_all, weights_all, first_all, second_all = ([], [], [], [])
    for group in range(REPS):
        narrow = weights[group].astype(jnp.bfloat16)
        keys_all.append(jnp.dot(inputs[group], narrow, preferred_element_type=jnp.float32).astype(jnp.bfloat16))
        gradient = lax.dot_general(inputs[group], cotangent[group], (((0,), (0,)), ((), ())), preferred_element_type=jnp.float32)
        moment_one = beta_one * first_moment[group] + (1.0 - beta_one) * gradient
        moment_two = beta_two * second_moment[group] + (1.0 - beta_two) * gradient * gradient
        stepped = weights[group] - inner_rate * (moment_one / (jnp.sqrt(moment_two) + adam_epsilon) + weight_decay * weights[group])
        frag_cols = lax.dynamic_slice_in_dim(stepped, frag_start, FRAG_W, 1) + pseudo_grad[group] - update
        stepped = lax.dynamic_update_slice(stepped, frag_cols, (zero_index, frag_start))
        weights_all.append(stepped)
        first_all.append(moment_one)
        second_all.append(moment_two)
    return (jnp.stack(keys_all), jnp.stack(weights_all), jnp.stack(first_all), jnp.stack(second_all), new_anchor, new_momentum)
```

```python
import jax
import jax.numpy as jnp
from jax import lax
from jax.experimental import pallas as pl
from jax.experimental.pallas import tpu as pltpu
from jax.sharding import PartitionSpec as P

MESH = pl.DeviceIdType.MESH

beta_one = 0.9
beta_two = 0.95
inner_rate = 0.002
weight_decay = 0.1
adam_epsilon = 1e-08
outer_rate = 0.7
outer_momentum = 0.9

RING = 4
TWO = 2
PEERS = 8
COMBOS = RING * TWO
SIDE = 256

GATHER_ONE = 0
GATHER_TWO = GATHER_ONE + TWO * 2 * 4
REDUCE_ONE = GATHER_TWO + COMBOS * 2 * 4
REDUCE_TWO = REDUCE_ONE + COMBOS * 2 * 4
GATHER_Z = REDUCE_TWO + TWO * 2 * 4
REDUCE_Z = GATHER_Z + 2
PSUM_ONE = REDUCE_Z + 2
PSUM_TWO = PSUM_ONE + PEERS
N_SEMS = PSUM_TWO + PEERS

TOP = pl.ds(0, SIDE // 2)
LOW = pl.ds(SIDE // 2, SIDE // 2)
ALL = pl.ds(0, SIDE)
ROWS = (ALL, ALL, TOP, LOW)
STEP = (1, 3, 1, 3)


def gray(j):
    return j + j // 2 - 2 * (j // 2) * (j % 2)


def body(
    x_hbm, c_hbm, w_hbm, p_hbm, proj_ref, grad_ref, delta_ref,
    xb, cb, ct, wf, wg, acc, far, up, down, relay, sums, far2, up2, down2, relay2, sums2,
    zs, zr, grad_t, pg, pr, dl, load_sem, ss, rs,
):
    fsdp = lax.axis_index("fsdp")
    rep = lax.axis_index("rep")
    x, y, z = fsdp // 8, (fsdp // 2) % 4, fsdp % 2

    def place(h, first, second, zz):
        dx, dy = (first, second) if h == 0 else (second, first)
        return ((x + dx) % 4) * 8 + ((y + dy) % 4) * 2 + zz

    loads = [
        pltpu.make_async_copy(w_hbm, wf, load_sem.at[0]),
        pltpu.make_async_copy(c_hbm, cb, load_sem.at[1]),
        pltpu.make_async_copy(p_hbm, pg, load_sem.at[2]),
    ]
    for load in loads:
        load.start()

    @pl.loop(0, 32)
    def _(i):
        columns = pl.ds(pl.multiple_of(i * SIDE, SIDE), SIDE)
        pltpu.make_async_copy(x_hbm.at[:, columns], xb.at[i], load_sem.at[3]).start()

    barrier = pltpu.get_barrier_semaphore()
    near = [place(0, 1, 0, z), place(0, 3, 0, z), place(0, 0, 1, z), place(0, 0, 3, z), place(0, 0, 0, 1 - z)]
    for device in near:
        pl.semaphore_signal(barrier, inc=1, device_id={"fsdp": device}, device_id_type=MESH)
    for i in range(1, PEERS):
        pl.semaphore_signal(barrier, inc=1, device_id={"rep": (rep + i) % PEERS}, device_id_type=MESH)

    def send(src, dst, sem, device, axis="fsdp"):
        return pltpu.make_async_remote_copy(
            src_ref=src, dst_ref=dst, send_sem=ss.at[sem], recv_sem=rs.at[sem],
            device_id={axis: device}, device_id_type=MESH,
        )

    def ring(h, second, kind):
        return place(h, 0, STEP[kind], z) if second else place(h, STEP[kind], 0, z)

    def piece(f, h, kind):
        return wg.at[f, h, ROWS[kind]]

    def gather_copy(f, h, sem, kind, second):
        return send(piece(f, h, kind), piece(f, h, kind), sem + kind, ring(h, second, kind))

    def one_sem(r, h):
        return GATHER_ONE + (r * 2 + h) * 4

    def two_sem(a, h):
        return GATHER_TWO + (a * 2 + h) * 4

    def reduce_one_sem(c, h):
        return REDUCE_ONE + (c * 2 + h) * 4

    def reduce_two_sem(zi, h):
        return REDUCE_TWO + (zi * 2 + h) * 4

    def project(f, h):
        acc[h] += jnp.dot(xb[f], wg[f, h], preferred_element_type=jnp.float32)

    def gather_step(a):
        r, j = a // RING, a % RING
        zz = (z + r) % 2
        first = gray(j)
        for h in range(2):
            f = place(h, first, 0, zz)
            sem = one_sem(r, h)

            @pl.when(j == 0)
            def _():
                @pl.when(r == 1)
                def _():
                    send(wg.at[f, h], wg.at[f, h], GATHER_Z + h, place(0, 0, 0, 1 - z)).wait_recv()

                gather_copy(f, h, sem, 0, False).start()
                gather_copy(f, h, sem, 1, False).start()

            @pl.when(j == 1)
            def _():
                gather_copy(f, h, sem, 1, False).wait_recv()
                gather_copy(f, h, sem, 3, False).start()

            @pl.when(j == 2)
            def _():
                gather_copy(f, h, sem, 0, False).wait_recv()
                gather_copy(f, h, sem, 2, False).start()

            @pl.when(j == 3)
            def _():
                gather_copy(f, h, sem, 2, False).wait_recv()
                gather_copy(f, h, sem, 3, False).wait_recv()

            gather_copy(f, h, two_sem(a, h), 0, True).start()
            gather_copy(f, h, two_sem(a, h), 1, True).start()

    def gather_own(a):
        r, j = a // RING, a % RING
        for h in range(2):
            project(place(h, gray(j), 0, (z + r) % 2), h)

    def gather_forward(a):
        r, j = a // RING, a % RING
        zz = (z + r) % 2
        first = gray(j)
        for h in range(2):
            sem = two_sem(a, h)
            above, below = place(h, first, 1, zz), place(h, first, 3, zz)
            gather_copy(above, h, sem, 1, True).wait_recv()
            gather_copy(above, h, sem, 3, True).start()
            gather_copy(below, h, sem, 0, True).wait_recv()
            gather_copy(below, h, sem, 2, True).start()
        for h in range(2):
            project(place(h, first, 1, zz), h)
            project(place(h, first, 3, zz), h)

    def gather_last(a):
        r, j = a // RING, a % RING
        for h in range(2):
            f = place(h, gray(j), 2, (z + r) % 2)
            gather_copy(f, h, two_sem(a, h), 2, True).wait_recv()
            gather_copy(f, h, two_sem(a, h), 3, True).wait_recv()
            project(f, h)

    def partial(f, h):
        return jnp.dot(ct[h], xb[f], preferred_element_type=jnp.float32)

    def ring_copy(src, dst, h, sem, kind, second):
        return send(src.at[ROWS[kind]], dst.at[ROWS[kind]], sem + kind, ring(h, second, kind))

    def widen(value):
        return value.astype(jnp.float32)

    def narrow(value):
        return value.astype(jnp.bfloat16)

    def reduce_far(c):
        zi, j = c // RING, c % RING
        zz = (z + 1 + zi) % 2
        for h in range(2):
            far[c, h] = narrow(partial(place(h, gray(3 - j), 2, zz), h))
            sem = reduce_one_sem(c, h)
            ring_copy(far.at[c, h], relay.at[c, h], h, sem, 2, True).start()
            ring_copy(far.at[c, h], relay.at[c, h], h, sem, 3, True).start()

    def reduce_near(c):
        zi, j = c // RING, c % RING
        zz = (z + 1 + zi) % 2
        first = gray(3 - j)
        for h in range(2):
            sem = reduce_one_sem(c, h)
            value = partial(place(h, first, 1, zz), h)
            ring_copy(far.at[c, h], relay.at[c, h], h, sem, 2, True).wait_recv()
            up[c, h, TOP] = narrow(value[: SIDE // 2] + widen(relay[c, h, TOP]))
            up[c, h, LOW] = narrow(value[SIDE // 2 :])
            ring_copy(up.at[c, h], sums.at[c, h, 0], h, sem, 0, True).start()
            value = partial(place(h, first, 3, zz), h)
            ring_copy(far.at[c, h], relay.at[c, h], h, sem, 3, True).wait_recv()
            down[c, h, TOP] = narrow(value[: SIDE // 2])
            down[c, h, LOW] = narrow(value[SIDE // 2 :] + widen(relay[c, h, LOW]))
            ring_copy(down.at[c, h], sums.at[c, h, 1], h, sem, 1, True).start()

    def reduce_own(c):
        zi, j = c // RING, c % RING
        zz = (z + 1 + zi) % 2
        for h in range(2):
            sem = reduce_one_sem(c, h)
            sem2 = reduce_two_sem(zi, h)
            value = partial(place(h, gray(3 - j), 0, zz), h)
            ring_copy(up.at[c, h], sums.at[c, h, 0], h, sem, 0, True).wait_recv()
            ring_copy(down.at[c, h], sums.at[c, h, 1], h, sem, 1, True).wait_recv()
            value = value + widen(sums[c, h, 0]) + widen(sums[c, h, 1])

            @pl.when(j == 0)
            def _():
                far2[zi, h] = narrow(value)
                ring_copy(far2.at[zi, h], relay2.at[zi, h], h, sem2, 2, False).start()
                ring_copy(far2.at[zi, h], relay2.at[zi, h], h, sem2, 3, False).start()

            @pl.when(j == 1)
            def _():
                ring_copy(far2.at[zi, h], relay2.at[zi, h], h, sem2, 3, False).wait_recv()
                down2[zi, h, TOP] = narrow(value[: SIDE // 2])
                down2[zi, h, LOW] = narrow(value[SIDE // 2 :] + widen(relay2[zi, h, LOW]))
                ring_copy(down2.at[zi, h], sums2.at[zi, h, 1], h, sem2, 1, False).start()

            @pl.when(j == 2)
            def _():
                ring_copy(far2.at[zi, h], relay2.at[zi, h], h, sem2, 2, False).wait_recv()
                up2[zi, h, TOP] = narrow(value[: SIDE // 2] + widen(relay2[zi, h, TOP]))
                up2[zi, h, LOW] = narrow(value[SIDE // 2 :])
                ring_copy(up2.at[zi, h], sums2.at[zi, h, 0], h, sem2, 0, False).start()

            @pl.when(j == 3)
            def _():
                ring_copy(up2.at[zi, h], sums2.at[zi, h, 0], h, sem2, 0, False).wait_recv()
                ring_copy(down2.at[zi, h], sums2.at[zi, h, 1], h, sem2, 1, False).wait_recv()
                total = value + widen(sums2[zi, h, 0]) + widen(sums2[zi, h, 1])

                @pl.when(zi == 0)
                def _():
                    zs[h] = total
                    send(zs.at[h], zr.at[h], REDUCE_Z + h, place(0, 0, 0, 1 - z)).start()

                @pl.when(zi == 1)
                def _():
                    grad_t[h] = total

    share = SIDE // PEERS

    def share_of(device):
        return pl.ds(pl.multiple_of(device * share, share), share)

    def psum_one(i):
        peer = (rep + i) % PEERS
        return send(pg.at[share_of(peer)], pr.at[rep], PSUM_ONE + i, peer, "rep")

    def psum_two(i):
        peer = (rep + i) % PEERS
        return send(dl.at[share_of(rep)], dl.at[share_of(rep)], PSUM_TWO + i, peer, "rep")

    loads[0].wait()
    for h in range(2):
        wg[fsdp, h] = wf[:, h * SIDE : (h + 1) * SIDE].astype(jnp.bfloat16)
    pl.semaphore_wait(barrier, len(near) + PEERS - 1)
    for h in range(2):
        send(wg.at[fsdp, h], wg.at[fsdp, h], GATHER_Z + h, place(0, 0, 0, 1 - z)).start()
    gather_step(0)
    loads[2].wait()
    for i in range(1, PEERS):
        psum_one(i).start()
    loads[1].wait()
    for h in range(2):
        half = cb[:, h * SIDE : (h + 1) * SIDE].astype(jnp.float32)
        ct[h] = half.T.astype(jnp.bfloat16)
    acc[...] = jnp.zeros_like(acc)
    pltpu.make_async_copy(xb, xb, load_sem.at[3]).wait()

    @pl.loop(0, COMBOS + 2)
    def _(k):
        @pl.when(k < COMBOS)
        def _():
            reduce_far(k)

            @pl.when(k > 0)
            def _():
                gather_step(k)

            gather_own(k)

        @pl.when((k >= 1) & (k < COMBOS + 1))
        def _():
            reduce_near(k - 1)
            gather_forward(k - 1)

        @pl.when(k >= 2)
        def _():
            reduce_own(k - 2)
            gather_last(k - 2)

        @pl.when(k == 2)
        def _():
            pr[rep] = pg[share_of(rep)]
            for i in range(1, PEERS):
                psum_one(i).wait_recv()
            dl[share_of(rep)] = jnp.sum(pr[...], axis=0)
            for i in range(1, PEERS):
                psum_two(i).start()

    proj_ref[...] = jnp.concatenate([acc[0], acc[1]], axis=1).astype(jnp.bfloat16)
    for h in range(2):
        send(zs.at[h], zr.at[h], REDUCE_Z + h, place(0, 0, 0, 1 - z)).wait_recv()
        grad_ref[:, h * SIDE : (h + 1) * SIDE] = (grad_t[h] + zr[h]).T
    for i in range(1, PEERS):
        peer = (rep + PEERS - i) % PEERS
        send(dl.at[share_of(peer)], dl.at[share_of(peer)], PSUM_TWO + i, peer, "rep").wait_recv()
    delta_ref[...] = dl[...]

    for i in range(1, PEERS):
        psum_one(i).wait_send()
        psum_two(i).wait_send()
    for h in range(2):
        send(wg.at[fsdp, h], wg.at[fsdp, h], GATHER_Z + h, place(0, 0, 0, 1 - z)).wait_send()
        send(zs.at[h], zr.at[h], REDUCE_Z + h, place(0, 0, 0, 1 - z)).wait_send()

    @pl.loop(0, COMBOS)
    def _(c):
        for h in range(2):
            for kind in range(4):
                gather_copy(fsdp, h, two_sem(c, h), kind, True).wait_send()
                ring_copy(far.at[c, h], relay.at[c, h], h, reduce_one_sem(c, h), kind, True).wait_send()

    @pl.loop(0, TWO)
    def _(r):
        for h in range(2):
            for kind in range(4):
                gather_copy(fsdp, h, one_sem(r, h), kind, False).wait_send()
                ring_copy(far2.at[r, h], relay2.at[r, h], h, reduce_two_sem(r, h), kind, False).wait_send()


def exchange(tokens, grads_in, master, pseudo):
    n, depth = tokens.shape
    rows, width = master.shape
    bf16, f32 = jnp.bfloat16, jnp.float32
    square = (SIDE, SIDE)
    flops = 4 * n * depth * width
    return pl.pallas_call(
        body,
        out_shape=[
            jax.ShapeDtypeStruct((n, width), bf16),
            jax.ShapeDtypeStruct((rows, width), f32),
            jax.ShapeDtypeStruct(pseudo.shape, f32),
        ],
        in_specs=[pl.BlockSpec(memory_space=pl.ANY)] * 4,
        out_specs=[pl.BlockSpec(memory_space=pltpu.VMEM)] * 3,
        scratch_shapes=[
            pltpu.VMEM((32, n, SIDE), bf16),
            pltpu.VMEM((n, width), bf16),
            pltpu.VMEM((2, SIDE, n), bf16),
            pltpu.VMEM((rows, width), f32),
            pltpu.VMEM((32, 2) + square, bf16),
            pltpu.VMEM((2, n, SIDE), f32),
            pltpu.VMEM((COMBOS, 2) + square, bf16),
            pltpu.VMEM((COMBOS, 2) + square, bf16),
            pltpu.VMEM((COMBOS, 2) + square, bf16),
            pltpu.VMEM((COMBOS, 2) + square, bf16),
            pltpu.VMEM((COMBOS, 2, 2) + square, bf16),
            pltpu.VMEM((TWO, 2) + square, bf16),
            pltpu.VMEM((TWO, 2) + square, bf16),
            pltpu.VMEM((TWO, 2) + square, bf16),
            pltpu.VMEM((TWO, 2) + square, bf16),
            pltpu.VMEM((TWO, 2, 2) + square, bf16),
            pltpu.VMEM((2,) + square, f32),
            pltpu.VMEM((2,) + square, f32),
            pltpu.VMEM((2,) + square, f32),
            pltpu.VMEM(pseudo.shape, f32),
            pltpu.VMEM((PEERS, SIDE // PEERS, pseudo.shape[1]), f32),
            pltpu.VMEM(pseudo.shape, f32),
            pltpu.SemaphoreType.DMA((4,)),
            pltpu.SemaphoreType.DMA((N_SEMS,)),
            pltpu.SemaphoreType.DMA((N_SEMS,)),
        ],
        compiler_params=pltpu.CompilerParams(
            collective_id=0, has_side_effects=True, vmem_limit_bytes=58 * 2**20
        ),
        cost_estimate=pl.CostEstimate(flops=flops, bytes_accessed=12 * 2**20, transcendentals=0),
    )(tokens, grads_in, master, pseudo)


def shards(
    inputs, cotangent, weights, first_moment, second_moment, pseudo_grad, anchor, momentum, fragment
):
    master = weights[0]
    frag_w = pseudo_grad.shape[2]
    frag_start = fragment[0] * frag_w
    zero_index = jnp.zeros((), jnp.int32)
    groups = lax.axis_size("rep")
    projected, gradient, summed = exchange(inputs[0], cotangent[0], master, pseudo_grad[0])
    mean_delta = summed / groups
    mom_frag = lax.dynamic_slice_in_dim(momentum, frag_start, frag_w, 1)
    new_mom_frag = outer_momentum * mom_frag + mean_delta
    update = outer_rate * (outer_momentum * new_mom_frag + mean_delta)
    anchor_frag = lax.dynamic_slice_in_dim(anchor, frag_start, frag_w, 1)
    new_anchor = lax.dynamic_update_slice(anchor, anchor_frag - update, (zero_index, frag_start))
    new_momentum = lax.dynamic_update_slice(momentum, new_mom_frag, (zero_index, frag_start))
    moment_one = beta_one * first_moment[0] + (1.0 - beta_one) * gradient
    moment_two = beta_two * second_moment[0] + (1.0 - beta_two) * gradient * gradient
    stepped = master - inner_rate * (
        moment_one / (jnp.sqrt(moment_two) + adam_epsilon) + weight_decay * master
    )
    frag_cols = lax.dynamic_slice_in_dim(stepped, frag_start, frag_w, 1) + pseudo_grad[0] - update
    stepped = lax.dynamic_update_slice(stepped, frag_cols, (zero_index, frag_start))
    return (
        projected[None],
        stepped[None],
        moment_one[None],
        moment_two[None],
        new_anchor,
        new_momentum,
    )


def solution(mesh):
    return jax.shard_map(
        shards,
        mesh=mesh,
        in_specs=(
            P("rep", "fsdp", None),
            P("rep", "fsdp", None),
            P("rep", "fsdp", None),
            P("rep", "fsdp", None),
            P("rep", "fsdp", None),
            P("rep", "fsdp", None),
            P("fsdp", None),
            P("fsdp", None),
            P(),
        ),
        out_specs=(
            P("rep", "fsdp", None),
            P("rep", "fsdp", None),
            P("rep", "fsdp", None),
            P("rep", "fsdp", None),
            P("fsdp", None),
            P("fsdp", None),
        ),
        check_vma=False,
    )
```

```python
import jax
import jax.numpy as jnp
from jax import lax
from jax.experimental import pallas as pl
from jax.experimental.pallas import tpu as pltpu
from jax.sharding import PartitionSpec as P

MESH = pl.DeviceIdType.MESH

beta_one = 0.9
beta_two = 0.95
inner_rate = 0.002
weight_decay = 0.1
adam_epsilon = 1e-08
outer_rate = 0.7
outer_momentum = 0.9

RING = 4
TWO = 2
PEERS = 8
COMBOS = RING * TWO
SIDE = 256
HALF = SIDE // 2
LAG = 3

GATHER_RING = 0
GATHER_CROSS = GATHER_RING + TWO * 2 * 4
TRADE = GATHER_CROSS + COMBOS * 2
TRADE_COT = TRADE + COMBOS * 2 * 2
REDUCE_CROSS = TRADE_COT + 2
REDUCE_RING = REDUCE_CROSS + COMBOS * 2
GATHER_Z = REDUCE_RING + TWO * 2 * 4
REDUCE_Z = GATHER_Z + 2
KEYS = REDUCE_Z + 2
PSUM_ONE = KEYS + 2
PSUM_TWO = PSUM_ONE + PEERS
N_SEMS = PSUM_TWO + PEERS

STEP = (1, 3, 1, 3)
OWN, CROSS, PAIR, PAIR_CROSS = range(4)


def gray(j):
    return j + j // 2 - 2 * (j // 2) * (j % 2)


def rows_of(kind, n):
    return (pl.ds(0, n), pl.ds(0, n), pl.ds(0, n // 2), pl.ds(n // 2, n // 2))[kind]


def body(
    x_hbm, c_hbm, w_hbm, p_hbm, proj_ref, grad_ref, delta_ref,
    xc, cb, ct, wf, wg, acc, acc_pair, keys, keys_in,
    cross, cross_in, far, up, down, relay, sums,
    zs, zr, grad_t, pg, pr, dl, load_sem, ss, rs,
):
    fsdp = lax.axis_index("fsdp")
    rep = lax.axis_index("rep")
    x, y, z = fsdp // 8, (fsdp // 2) % 4, fsdp % 2
    tokens, width = c_hbm.shape

    def along(at, who):
        pair = at + 1 - 2 * (at % 2)
        return (at, 3 - at, pair, 3 - pair)[who]

    def place(h, who, step, zz):
        if h == 0:
            return along(x, who) * 8 + ((y + step) % 4) * 2 + zz
        return ((x + step) % 4) * 8 + along(y, who) * 2 + zz

    other_z = fsdp + 1 - 2 * z

    def send(src, dst, sem, device, axis="fsdp"):
        return pltpu.make_async_remote_copy(
            src_ref=src, dst_ref=dst, send_sem=ss.at[sem], recv_sem=rs.at[sem],
            device_id={axis: device}, device_id_type=MESH,
        )

    def gather_round(a):
        return a // RING, a % RING, (z + a // RING) % 2, gray(a % RING)

    def reduce_round(c):
        return c // RING, c % RING, (z + 1 + c // RING) % 2, gray(3 - c % RING)

    load_w = pltpu.make_async_copy(w_hbm, wf, load_sem.at[0])
    load_c = pltpu.make_async_copy(c_hbm, cb.at[0], load_sem.at[1])
    load_p = pltpu.make_async_copy(p_hbm, pg, load_sem.at[2])
    load_w.start()
    load_c.start()
    load_p.start()

    def block(f, h):
        return x_hbm.at[:, pl.ds(pl.multiple_of(f * SIDE + h * HALF, HALF), HALF)]

    @pl.loop(0, COMBOS)
    def _(c):
        _, _, zz, step = reduce_round(c)
        for h in range(2):
            for who in (CROSS, OWN):
                f = place(h, who, step, zz)
                pltpu.make_async_copy(block(f, h), xc.at[f, h, pl.ds(0, tokens)], load_sem.at[3]).start()

    barrier = pltpu.get_barrier_semaphore()
    near = [place(0, PAIR, 0, z), place(0, CROSS, 0, z), place(1, PAIR, 0, z), place(1, CROSS, 0, z), other_z]
    for device in near:
        pl.semaphore_signal(barrier, inc=1, device_id={"fsdp": device}, device_id_type=MESH)
    for i in range(1, PEERS):
        pl.semaphore_signal(barrier, inc=1, device_id={"rep": (rep + i) % PEERS}, device_id_type=MESH)

    def trade_cot(h):
        return send(c_hbm, cb.at[1 + h], TRADE_COT + h, place(h, PAIR, 0, z))

    def trade_start(c):
        _, _, zz, step = reduce_round(c)
        for h in range(2):
            for i, who in enumerate((PAIR_CROSS, PAIR)):
                f = place(h, who, step, zz)
                sem = TRADE + (c * 2 + h) * 2 + i
                send(block(f, h), xc.at[f, h, pl.ds(tokens, tokens)], sem, place(h, PAIR, 0, z)).start()

    def trade_wait(c, h, i):
        _, _, zz, step = reduce_round(c)
        f = place(h, (CROSS, OWN)[i], step, zz)
        sem = TRADE + (c * 2 + h) * 2 + i
        send(block(f, h), xc.at[f, h, pl.ds(tokens, tokens)], sem, place(h, PAIR, 0, z)).wait_recv()

    def gather_ring(f, h, r, kind):
        part = wg.at[f, h, rows_of(kind, HALF)]
        return send(part, part, GATHER_RING + (r * 2 + h) * 4 + kind, place(h, OWN, STEP[kind], z))

    def gather_cross(f, h, a):
        return send(wg.at[f, h], wg.at[f, h], GATHER_CROSS + a * 2 + h, place(h, CROSS, 0, z))

    def gather_z(f, h):
        return send(wg.at[f, h], wg.at[f, h], GATHER_Z + h, other_z)

    def gather_step(a):
        r, j, zz, step = gather_round(a)
        for h in range(2):
            f = place(h, OWN, step, zz)

            @pl.when(j == 0)
            def _():
                @pl.when(r == 1)
                def _():
                    gather_z(f, h).wait_recv()

                gather_ring(f, h, r, 0).start()
                gather_ring(f, h, r, 1).start()

            @pl.when(j == 1)
            def _():
                gather_ring(f, h, r, 1).wait_recv()
                gather_ring(f, h, r, 3).start()

            @pl.when(j == 2)
            def _():
                gather_ring(f, h, r, 0).wait_recv()
                gather_ring(f, h, r, 2).start()

            @pl.when(j == 3)
            def _():
                gather_ring(f, h, r, 2).wait_recv()
                gather_ring(f, h, r, 3).wait_recv()

            gather_cross(f, h, a).start()

    def project(c):
        _, _, zz, step = reduce_round(c)
        for h in range(2):
            here, there = place(h, OWN, step, zz), place(h, CROSS, step, zz)
            gather_cross(there, h, COMBOS - 1 - c).wait_recv()
            value = jnp.dot(xc[here, h], wg[here, h], preferred_element_type=jnp.float32)
            value += jnp.dot(xc[there, h], wg[there, h], preferred_element_type=jnp.float32)
            acc[...] += value[:tokens]
            acc_pair[h] += value[tokens:]

    def keys_copy(h):
        return send(keys.at[h], keys_in.at[h], KEYS + h, place(h, PAIR, 0, z))

    def partial(f, h):
        return jnp.dot(ct[h], xc[f, h], preferred_element_type=jnp.float32)

    def widen(value):
        return value.astype(jnp.float32)

    def narrow(value):
        return value.astype(jnp.bfloat16)

    def reduce_cross(c, h):
        return send(cross.at[c, h], cross_in.at[c, h], REDUCE_CROSS + c * 2 + h, place(h, CROSS, 0, z))

    def reduce_ring(src, dst, zi, h, kind):
        rows = rows_of(kind, width)
        sem = REDUCE_RING + (zi * 2 + h) * 4 + kind
        return send(src.at[zi, h, rows], dst.at[rows], sem, place(h, OWN, STEP[kind], z))

    def relay_copy(zi, h, kind):
        return reduce_ring(far, relay.at[zi, h], zi, h, kind)

    def up_copy(zi, h):
        return reduce_ring(up, sums.at[zi, h, 0], zi, h, 0)

    def down_copy(zi, h):
        return reduce_ring(down, sums.at[zi, h, 1], zi, h, 1)

    def reduce_z(h):
        return send(zs.at[h], zr.at[h], REDUCE_Z + h, other_z)

    def reduce_first(c):
        _, _, zz, step = reduce_round(c)
        for h in range(2):
            trade_wait(c, h, 0)
            trade_wait(c, h, 1)
            cross[c, h] = narrow(partial(place(h, CROSS, step, zz), h))
            reduce_cross(c, h).start()

    def reduce_second(c):
        zi, j, zz, step = reduce_round(c)
        top, low = slice(0, width // 2), slice(width // 2, width)
        for h in range(2):
            value = partial(place(h, OWN, step, zz), h)
            reduce_cross(c, h).wait_recv()
            value = value + widen(cross_in[c, h])

            @pl.when(j == 0)
            def _():
                far[zi, h] = narrow(value)
                relay_copy(zi, h, 2).start()
                relay_copy(zi, h, 3).start()

            @pl.when(j == 1)
            def _():
                relay_copy(zi, h, 3).wait_recv()
                down[zi, h, top] = narrow(value[top])
                down[zi, h, low] = narrow(value[low] + widen(relay[zi, h, low]))
                down_copy(zi, h).start()

            @pl.when(j == 2)
            def _():
                relay_copy(zi, h, 2).wait_recv()
                up[zi, h, top] = narrow(value[top] + widen(relay[zi, h, top]))
                up[zi, h, low] = narrow(value[low])
                up_copy(zi, h).start()

            @pl.when(j == 3)
            def _():
                up_copy(zi, h).wait_recv()
                down_copy(zi, h).wait_recv()
                total = value + widen(sums[zi, h, 0]) + widen(sums[zi, h, 1])

                @pl.when(zi == 0)
                def _():
                    zs[h] = total
                    reduce_z(h).start()

                @pl.when(zi == 1)
                def _():
                    grad_t[h] = total

    share = SIDE // PEERS

    def share_of(device):
        return pl.ds(pl.multiple_of(device * share, share), share)

    def psum_one(i):
        peer = (rep + i) % PEERS
        return send(pg.at[share_of(peer)], pr.at[rep], PSUM_ONE + i, peer, "rep")

    def psum_two(i):
        peer = (rep + i) % PEERS
        return send(dl.at[share_of(rep)], dl.at[share_of(rep)], PSUM_TWO + i, peer, "rep")

    pl.semaphore_wait(barrier, len(near) + PEERS - 1)
    trade_cot(0).start()
    trade_cot(1).start()
    trade_start(0)
    load_w.wait()
    for h in range(2):
        wg[fsdp, h] = narrow(wf[h * HALF : (h + 1) * HALF])
    for h in range(2):
        gather_z(fsdp, h).start()
    gather_step(0)
    trade_start(1)
    load_p.wait()
    for i in range(1, PEERS):
        psum_one(i).start()
    acc[...] = jnp.zeros_like(acc)
    acc_pair[...] = jnp.zeros_like(acc_pair)
    load_c.wait()
    turned = narrow(widen(cb[0]).T)
    ct[0, :, 0:tokens] = turned
    ct[1, :, 0:tokens] = turned
    pltpu.make_async_copy(
        xc.at[pl.ds(0, 16), :, pl.ds(0, tokens)], xc.at[pl.ds(0, 16), :, pl.ds(0, tokens)], load_sem.at[3]
    ).wait()

    @pl.loop(1, COMBOS + LAG + 1)
    def _(k):
        @pl.when(k < COMBOS)
        def _():
            gather_step(k)

        @pl.when((k >= LAG) & (k < COMBOS + 1))
        def _():
            trade_start(k - LAG + 2)

        @pl.when(k == 2)
        def _():
            pr[rep] = pg[share_of(rep)]
            for i in range(1, PEERS):
                psum_one(i).wait_recv()
            dl[share_of(rep)] = jnp.sum(pr[...], axis=0)
            for i in range(1, PEERS):
                psum_two(i).start()
            for h in range(2):
                trade_cot(h).wait_recv()
                ct[h, :, tokens : 2 * tokens] = narrow(widen(cb[1 + h]).T)

        @pl.when((k >= LAG) & (k < COMBOS + LAG))
        def _():
            reduce_first(k - LAG)

        @pl.when(k >= LAG + 1)
        def _():
            reduce_second(k - LAG - 1)

        @pl.when((k >= LAG + 3) & (k < COMBOS + LAG))
        def _():
            project(k - LAG)

        @pl.when((k >= LAG + 4) & (k < LAG + 7))
        def _():
            project(LAG + 6 - k)

        @pl.when(k == COMBOS + LAG - 1)
        def _():
            for h in range(2):
                keys[h] = narrow(acc_pair[h])
                keys_copy(h).start()

    for h in range(2):
        reduce_z(h).wait_recv()
        grad_ref[h * HALF : (h + 1) * HALF] = (grad_t[h] + zr[h]).T
    for i in range(1, PEERS):
        peer = (rep + PEERS - i) % PEERS
        send(dl.at[share_of(peer)], dl.at[share_of(peer)], PSUM_TWO + i, peer, "rep").wait_recv()
    delta_ref[...] = dl[...]
    keys_copy(0).wait_recv()
    keys_copy(1).wait_recv()
    proj_ref[...] = narrow(acc[...] + widen(keys_in[0]) + widen(keys_in[1]))

    for i in range(1, PEERS):
        psum_one(i).wait_send()
        psum_two(i).wait_send()
    for h in range(2):
        gather_z(fsdp, h).wait_send()
        reduce_z(h).wait_send()
        keys_copy(h).wait_send()
        trade_cot(h).wait_send()

    @pl.loop(0, COMBOS)
    def _(c):
        for h in range(2):
            gather_cross(fsdp, h, c).wait_send()
            reduce_cross(c, h).wait_send()
            for i in range(2):
                sem = TRADE + (c * 2 + h) * 2 + i
                send(block(0, h), xc.at[fsdp, h, pl.ds(tokens, tokens)], sem, other_z).wait_send()

    @pl.loop(0, TWO)
    def _(r):
        for h in range(2):
            for kind in range(4):
                gather_ring(fsdp, h, r, kind).wait_send()
                reduce_ring(far, relay.at[r, h], r, h, kind).wait_send()


def exchange(tokens, grads_in, master, pseudo):
    n, depth = tokens.shape
    rows, width = master.shape
    bf16, f32 = jnp.bfloat16, jnp.float32
    tall = (width, HALF)
    flops = 4 * n * depth * width
    return pl.pallas_call(
        body,
        out_shape=[
            jax.ShapeDtypeStruct((n, width), bf16),
            jax.ShapeDtypeStruct((rows, width), f32),
            jax.ShapeDtypeStruct(pseudo.shape, f32),
        ],
        in_specs=[pl.BlockSpec(memory_space=pl.ANY)] * 4,
        out_specs=[pl.BlockSpec(memory_space=pltpu.VMEM)] * 3,
        scratch_shapes=[
            pltpu.VMEM((32, 2, 2 * n, HALF), bf16),
            pltpu.VMEM((3, n, width), bf16),
            pltpu.VMEM((2, width, 2 * n), bf16),
            pltpu.VMEM((rows, width), f32),
            pltpu.VMEM((32, 2, HALF, width), bf16),
            pltpu.VMEM((n, width), f32),
            pltpu.VMEM((2, n, width), f32),
            pltpu.VMEM((2, n, width), bf16),
            pltpu.VMEM((2, n, width), bf16),
            pltpu.VMEM((COMBOS, 2) + tall, bf16),
            pltpu.VMEM((COMBOS, 2) + tall, bf16),
            pltpu.VMEM((TWO, 2) + tall, bf16),
            pltpu.VMEM((TWO, 2) + tall, bf16),
            pltpu.VMEM((TWO, 2) + tall, bf16),
            pltpu.VMEM((TWO, 2) + tall, bf16),
            pltpu.VMEM((TWO, 2, 2) + tall, bf16),
            pltpu.VMEM((2,) + tall, f32),
            pltpu.VMEM((2,) + tall, f32),
            pltpu.VMEM((2,) + tall, f32),
            pltpu.VMEM(pseudo.shape, f32),
            pltpu.VMEM((PEERS, SIDE // PEERS, pseudo.shape[1]), f32),
            pltpu.VMEM(pseudo.shape, f32),
            pltpu.SemaphoreType.DMA((4,)),
            pltpu.SemaphoreType.DMA((N_SEMS,)),
            pltpu.SemaphoreType.DMA((N_SEMS,)),
        ],
        compiler_params=pltpu.CompilerParams(
            collective_id=0, has_side_effects=True, vmem_limit_bytes=58 * 2**20
        ),
        cost_estimate=pl.CostEstimate(flops=flops, bytes_accessed=12 * 2**20, transcendentals=0),
    )(tokens, grads_in, master, pseudo)


def shards(
    inputs, cotangent, weights, first_moment, second_moment, pseudo_grad, anchor, momentum, fragment
):
    master = weights[0]
    frag_w = pseudo_grad.shape[2]
    frag_start = fragment[0] * frag_w
    zero_index = jnp.zeros((), jnp.int32)
    groups = lax.axis_size("rep")
    projected, gradient, summed = exchange(inputs[0], cotangent[0], master, pseudo_grad[0])
    mean_delta = summed / groups
    mom_frag = lax.dynamic_slice_in_dim(momentum, frag_start, frag_w, 1)
    new_mom_frag = outer_momentum * mom_frag + mean_delta
    update = outer_rate * (outer_momentum * new_mom_frag + mean_delta)
    anchor_frag = lax.dynamic_slice_in_dim(anchor, frag_start, frag_w, 1)
    new_anchor = lax.dynamic_update_slice(anchor, anchor_frag - update, (zero_index, frag_start))
    new_momentum = lax.dynamic_update_slice(momentum, new_mom_frag, (zero_index, frag_start))
    moment_one = beta_one * first_moment[0] + (1.0 - beta_one) * gradient
    moment_two = beta_two * second_moment[0] + (1.0 - beta_two) * gradient * gradient
    stepped = master - inner_rate * (
        moment_one / (jnp.sqrt(moment_two) + adam_epsilon) + weight_decay * master
    )
    frag_cols = lax.dynamic_slice_in_dim(stepped, frag_start, frag_w, 1) + pseudo_grad[0] - update
    stepped = lax.dynamic_update_slice(stepped, frag_cols, (zero_index, frag_start))
    return (
        projected[None],
        stepped[None],
        moment_one[None],
        moment_two[None],
        new_anchor,
        new_momentum,
    )


def solution(mesh):
    return jax.shard_map(
        shards,
        mesh=mesh,
        in_specs=(
            P("rep", "fsdp", None),
            P("rep", "fsdp", None),
            P("rep", "fsdp", None),
            P("rep", "fsdp", None),
            P("rep", "fsdp", None),
            P("rep", "fsdp", None),
            P("fsdp", None),
            P("fsdp", None),
            P(),
        ),
        out_specs=(
            P("rep", "fsdp", None),
            P("rep", "fsdp", None),
            P("rep", "fsdp", None),
            P("rep", "fsdp", None),
            P("fsdp", None),
            P("fsdp", None),
        ),
        check_vma=False,
    )
```

```python
import jax
import jax.numpy as jnp
from jax import lax
from jax.experimental import pallas as pl
from jax.experimental.pallas import tpu as pltpu
from jax.sharding import PartitionSpec as P

MESH = pl.DeviceIdType.MESH

beta_one = 0.9
beta_two = 0.95
inner_rate = 0.002
weight_decay = 0.1
adam_epsilon = 1e-08
outer_rate = 0.7
outer_momentum = 0.9

RING = 4
TWO = 2
PEERS = 8
COMBOS = RING * TWO
SIDE = 256
HALF = SIDE // 2
COT_PARTS = 3
FINISH_STEPS = 2

OWN, PAIR, FAR, CROSS = range(4)
GATHER_ORDER = (OWN, CROSS, PAIR, FAR)
VIA = (CROSS, CROSS)
BY_Z = (PAIR, FAR)
Z_DTYPE = jnp.float32

GATHER_RING = 0
GATHER_CROSS = GATHER_RING + TWO * RING * 2
GATHER_Z = GATHER_CROSS + TWO * RING * 2
TRADE = GATHER_Z + RING * 2
TRADE_COT = TRADE + COMBOS * 2 * 2
REDUCE_CROSS = TRADE_COT + 2 * COT_PARTS
REDUCE_RING = REDUCE_CROSS + COMBOS * 2
REDUCE_Z = REDUCE_RING + TWO * 2 * 3
KEYS = REDUCE_Z + 2
PSUM_ONE = KEYS + 2
PSUM_TWO = PSUM_ONE + PEERS
N_SEMS = PSUM_TWO + PEERS

PLAN = (
    "C1", "G1", "T0", "G2", "C2", "G3", "T1", "G4", "T2", "T3", "L0", "W0", "T4", "G5", "F0", "T5",
    "F1", "S0", "F2", "F3", "P1", "S1", "R0", "P3", "S2", "G6", "T6", "G7", "P4", "F4", "P5", "S3",
    "T7", "F5", "P2", "F6", "P6", "P0", "P7", "K0", "S4", "S5", "S6", "F7", "S7",
)


def flip(at, where):
    return (at, at + 1 - 2 * (at % 2), (at + 2) % 4, 3 - at)[where]


def body(
    x_hbm, c_hbm, w_hbm, p_hbm, proj_ref, grad_ref, delta_ref,
    xc, cb, ct, wf, wg, acc, acc_pair, keys, keys_in,
    cross, cross_in, around, around_in,
    zs, zr, grad_t, pg, pr, dl, load_sem, ss, rs,
):
    fsdp = lax.axis_index("fsdp")
    rep = lax.axis_index("rep")
    x, y, z = fsdp // 8, (fsdp // 2) % 4, fsdp % 2
    tokens, width = c_hbm.shape

    def place(h, first, second, zz):
        dx, dy = (first, second) if h == 0 else (second, first)
        return flip(x, dx) * 8 + flip(y, dy) * 2 + zz

    other_z = fsdp + 1 - 2 * z

    def send(src, dst, sem, device, axis="fsdp"):
        return pltpu.make_async_remote_copy(
            src_ref=src, dst_ref=dst, send_sem=ss.at[sem], recv_sem=rs.at[sem],
            device_id={axis: device}, device_id_type=MESH,
        )

    def reduce_round(c):
        zi, j = divmod(c, RING)
        other = PAIR + CROSS - VIA[zi]
        return zi, j, (z + 1 + zi) % 2, (FAR, VIA[zi], other, OWN)[j]

    load_w = pltpu.make_async_copy(w_hbm, wf, load_sem.at[0])
    load_c = pltpu.make_async_copy(c_hbm, cb.at[0], load_sem.at[1])
    load_p = pltpu.make_async_copy(p_hbm, pg, load_sem.at[2])
    load_w.start()
    load_c.start()
    load_p.start()

    barrier = pltpu.get_barrier_semaphore()
    near = [place(0, PAIR, OWN, z), place(0, CROSS, OWN, z), place(1, PAIR, OWN, z), place(1, CROSS, OWN, z), other_z]
    for device in near:
        pl.semaphore_signal(barrier, inc=1, device_id={"fsdp": device}, device_id_type=MESH)
    for i in range(1, PEERS):
        pl.semaphore_signal(barrier, inc=1, device_id={"rep": (rep + i) % PEERS}, device_id_type=MESH)

    def block(f, h):
        return x_hbm.at[:, pl.ds(pl.multiple_of(f * SIDE + h * HALF, HALF), HALF)]

    for c in range(COMBOS):
        _, _, zz, there = reduce_round(c)
        for h in range(2):
            for who in (CROSS, OWN):
                f = place(h, who, there, zz)
                pltpu.make_async_copy(block(f, h), xc.at[f, h, pl.ds(0, tokens)], load_sem.at[3]).start()

    def trade_cot(h, part):
        rows = pl.ds(part * HALF, HALF)
        return send(c_hbm.at[rows], cb.at[1 + h, rows], TRADE_COT + h * COT_PARTS + part, place(h, PAIR, OWN, z))

    def cot_start(part):
        for h in range(2):
            trade_cot(h, part).start()

    def cot_wait(_):
        for h in range(2):
            for part in range(COT_PARTS):
                trade_cot(h, part).wait_recv()
            ct[h, :, tokens : 2 * tokens] = narrow(widen(cb[1 + h]).T)

    def trade(c, h, i, who):
        _, _, zz, there = reduce_round(c)
        f = place(h, who, there, zz)
        sem = TRADE + (c * 2 + h) * 2 + i
        return send(block(f, h), xc.at[f, h, pl.ds(tokens, tokens)], sem, place(h, PAIR, OWN, z))

    def trade_start(c):
        for h in range(2):
            trade(c, h, 0, FAR).start()
            trade(c, h, 1, PAIR).start()

    arrived = set()

    def need(c, h, i):
        if (c, h, i) not in arrived:
            trade(c, h, i, (CROSS, OWN)[i]).wait_recv()
            arrived.add((c, h, i))

    def gather_ring(r, h, f, where, to):
        return send(wg.at[f, h], wg.at[f, h], GATHER_RING + (r * RING + where) * 2 + h, place(h, OWN, to, z))

    def gather_cross(r, h, f, where):
        return send(wg.at[f, h], wg.at[f, h], GATHER_CROSS + (r * RING + where) * 2 + h, place(h, CROSS, OWN, z))

    def gather_z(h, f, where):
        return send(wg.at[f, h], wg.at[f, h], GATHER_Z + where * 2 + h, other_z)

    def gather_step(a):
        r, j = divmod(a, RING)
        where = GATHER_ORDER[j]
        for h in range(2):
            f = place(h, OWN, where, (z + r) % 2)
            if r == 1 and (where == OWN or where in BY_Z):
                gather_z(h, f, where).wait_recv()
            elif where != OWN:
                gather_ring(r, h, f, where, PAIR).wait_recv()
            if where == OWN:
                for to in (PAIR, CROSS):
                    if r == 0 or to not in BY_Z:
                        gather_ring(r, h, f, to, to).start()
            elif where == CROSS and (r == 0 or FAR not in BY_Z):
                gather_ring(r, h, f, FAR, PAIR + CROSS - where).start()
            if r == 0 and (where == OWN or where in BY_Z):
                gather_z(h, f, where).start()
            gather_cross(r, h, f, where).start()

    seen = []

    def project(c):
        zi, _, zz, there = reduce_round(c)
        for h in range(2):
            mine, crossed = place(h, OWN, there, zz), place(h, CROSS, there, zz)
            need(c, h, 0)
            need(c, h, 1)
            gather_cross(1 - zi, h, crossed, there).wait_recv()
            value = jnp.dot(xc[mine, h], wg[mine, h], preferred_element_type=jnp.float32)
            value += jnp.dot(xc[crossed, h], wg[crossed, h], preferred_element_type=jnp.float32)
            acc[...] = value[:tokens] + acc[...] if seen else value[:tokens]
            acc_pair[h] = value[tokens:] + acc_pair[h] if len(seen) > 1 else value[tokens:]
            seen.append(c)

    def keys_copy(h):
        return send(keys.at[h], keys_in.at[h], KEYS + h, place(h, PAIR, OWN, z))

    def keys_start(_):
        for h in range(2):
            keys[h] = narrow(acc_pair[h])
            keys_copy(h).start()

    def partial(f, h):
        return jnp.dot(ct[h], xc[f, h], preferred_element_type=jnp.float32)

    def widen(value):
        return value.astype(jnp.float32)

    def narrow(value):
        return value.astype(jnp.bfloat16)

    def reduce_cross(c, h):
        return send(cross.at[c, h], cross_in.at[c, h], REDUCE_CROSS + c * 2 + h, place(h, CROSS, OWN, z))

    def reduce_ring(zi, h, j, to):
        slot = (zi, h, j)
        return send(around.at[slot], around_in.at[slot], REDUCE_RING + (zi * 2 + h) * 3 + j, place(h, OWN, to, z))

    def reduce_z(h):
        return send(zs.at[h], zr.at[h], REDUCE_Z + h, other_z)

    def reduce_first(c):
        _, _, zz, there = reduce_round(c)
        for h in range(2):
            need(c, h, 0)
            cross[c, h] = narrow(partial(place(h, CROSS, there, zz), h))
            reduce_cross(c, h).start()

    def reduce_second(c):
        zi, j, zz, there = reduce_round(c)
        for h in range(2):
            need(c, h, 1)
            value = partial(place(h, OWN, there, zz), h)
            reduce_cross(c, h).wait_recv()
            value = value + widen(cross_in[c, h])
            if j == 2:
                reduce_ring(zi, h, 0, PAIR).wait_recv()
                value = value + widen(around_in[zi, h, 0])
            if j < 3:
                around[zi, h, j] = narrow(value)
                reduce_ring(zi, h, j, VIA[zi] if j == 0 else there).start()
            else:
                for i in (1, 2):
                    reduce_ring(zi, h, i, PAIR).wait_recv()
                    value = value + widen(around_in[zi, h, i])
                if zi == 0:
                    zs[h] = value.astype(Z_DTYPE)
                    reduce_z(h).start()
                else:
                    grad_t[h] = value

    share = SIDE // PEERS

    def share_of(device):
        return pl.ds(pl.multiple_of(device * share, share), share)

    def psum_one(i):
        peer = (rep + i) % PEERS
        return send(pg.at[share_of(peer)], pr.at[rep], PSUM_ONE + i, peer, "rep")

    def psum_two(i):
        peer = (rep + i) % PEERS
        return send(dl.at[share_of(rep)], dl.at[share_of(rep)], PSUM_TWO + i, peer, "rep")

    def psum_turn(_):
        pr[rep] = pg[share_of(rep)]
        for i in range(1, PEERS):
            psum_one(i).wait_recv()
        dl[share_of(rep)] = jnp.sum(pr[...], axis=0)
        for i in range(1, PEERS):
            psum_two(i).start()

    pl.semaphore_wait(barrier, len(near) + PEERS - 1)
    cot_start(0)
    load_w.wait()
    for h in range(2):
        wg[fsdp, h] = narrow(wf[h * HALF : (h + 1) * HALF])
    gather_step(0)
    load_p.wait()
    for i in range(1, PEERS):
        psum_one(i).start()
    load_c.wait()
    turned = narrow(widen(cb[0]).T)
    ct[0, :, 0:tokens] = turned
    ct[1, :, 0:tokens] = turned
    some = xc.at[pl.ds(0, 16), :, pl.ds(0, tokens)]
    loaded = pltpu.make_async_copy(some, some, load_sem.at[3])

    steps = dict(
        C=cot_start, W=cot_wait, G=gather_step, T=trade_start, P=project, K=keys_start,
        F=reduce_first, S=reduce_second, R=psum_turn, L=lambda _: loaded.wait(),
    )
    for step in PLAN:
        steps[step[0]](int(step[1]))

    for h in range(2):
        reduce_z(h).wait_recv()
        grad_ref[h * HALF : (h + 1) * HALF] = (grad_t[h] + widen(zr[h])).T
    for i in range(1, PEERS):
        peer = (rep + PEERS - i) % PEERS
        send(dl.at[share_of(peer)], dl.at[share_of(peer)], PSUM_TWO + i, peer, "rep").wait_recv()
    delta_ref[...] = dl[...]
    keys_copy(0).wait_recv()
    keys_copy(1).wait_recv()
    proj_ref[...] = narrow(acc[...] + widen(keys_in[0]) + widen(keys_in[1]))

    for i in range(1, PEERS):
        psum_one(i).wait_send()
        psum_two(i).wait_send()
    for h in range(2):
        reduce_z(h).wait_send()
        keys_copy(h).wait_send()
        for part in range(COT_PARTS):
            trade_cot(h, part).wait_send()
        for where in (OWN,) + BY_Z:
            gather_z(h, fsdp, where).wait_send()
        for where in range(RING):
            for r in range(TWO):
                gather_cross(r, h, fsdp, where).wait_send()
                if where != OWN and (r == 0 or where not in BY_Z):
                    gather_ring(r, h, fsdp, where, PAIR).wait_send()
        for zi in range(TWO):
            for j in range(3):
                reduce_ring(zi, h, j, PAIR).wait_send()
        for c in range(COMBOS):
            reduce_cross(c, h).wait_send()
            trade(c, h, 0, OWN).wait_send()
            trade(c, h, 1, OWN).wait_send()


def exchange(tokens, grads_in, master, pseudo):
    n, depth = tokens.shape
    rows, width = master.shape
    bf16, f32 = jnp.bfloat16, jnp.float32
    tall = (width, HALF)
    flops = 4 * n * depth * width
    return pl.pallas_call(
        body,
        out_shape=[
            jax.ShapeDtypeStruct((n, width), bf16),
            jax.ShapeDtypeStruct((rows, width), f32),
            jax.ShapeDtypeStruct(pseudo.shape, f32),
        ],
        in_specs=[pl.BlockSpec(memory_space=pl.ANY)] * 4,
        out_specs=[pl.BlockSpec(memory_space=pltpu.VMEM)] * 3,
        scratch_shapes=[
            pltpu.VMEM((32, 2, 2 * n, HALF), bf16),
            pltpu.VMEM((3, n, width), bf16),
            pltpu.VMEM((2, width, 2 * n), bf16),
            pltpu.VMEM((rows, width), f32),
            pltpu.VMEM((32, 2, HALF, width), bf16),
            pltpu.VMEM((n, width), f32),
            pltpu.VMEM((2, n, width), f32),
            pltpu.VMEM((2, n, width), bf16),
            pltpu.VMEM((2, n, width), bf16),
            pltpu.VMEM((COMBOS, 2) + tall, bf16),
            pltpu.VMEM((COMBOS, 2) + tall, bf16),
            pltpu.VMEM((TWO, 2, 3) + tall, bf16),
            pltpu.VMEM((TWO, 2, 3) + tall, bf16),
            pltpu.VMEM((2,) + tall, Z_DTYPE),
            pltpu.VMEM((2,) + tall, Z_DTYPE),
            pltpu.VMEM((2,) + tall, f32),
            pltpu.VMEM(pseudo.shape, f32),
            pltpu.VMEM((PEERS, SIDE // PEERS, pseudo.shape[1]), f32),
            pltpu.VMEM(pseudo.shape, f32),
            pltpu.SemaphoreType.DMA((4,)),
            pltpu.SemaphoreType.DMA((N_SEMS,)),
            pltpu.SemaphoreType.DMA((N_SEMS,)),
        ],
        compiler_params=pltpu.CompilerParams(
            collective_id=0, has_side_effects=True, vmem_limit_bytes=58 * 2**20
        ),
        cost_estimate=pl.CostEstimate(flops=flops, bytes_accessed=12 * 2**20, transcendentals=0),
    )(tokens, grads_in, master, pseudo)


def finish_body(
    frag_ref, keys_ref, grad_ref, delta_ref, w_ref, one_ref, two_ref, pseudo_ref, anchor_ref, mom_ref,
    keys_out, w_out, one_out, two_out, anchor_out, mom_out,
):
    frag = frag_ref[0]
    keys_out[...] = keys_ref[...]
    frag_w = delta_ref.shape[1]
    mean_delta = delta_ref[...] / PEERS
    pseudo = pseudo_ref[...]
    for q in range(w_ref.shape[1] // frag_w):
        columns = slice(q * frag_w, (q + 1) * frag_w)
        here = frag == q
        momentum, anchor = mom_ref[:, columns], anchor_ref[:, columns]
        new_momentum = outer_momentum * momentum + mean_delta
        update = outer_rate * (outer_momentum * new_momentum + mean_delta)
        mom_out[:, columns] = jnp.where(here, new_momentum, momentum)
        anchor_out[:, columns] = jnp.where(here, anchor - update, anchor)
        master, gradient = w_ref[:, columns], grad_ref[:, columns]
        moment_one = beta_one * one_ref[:, columns] + (1.0 - beta_one) * gradient
        moment_two = beta_two * two_ref[:, columns] + (1.0 - beta_two) * gradient * gradient
        one_out[:, columns] = moment_one
        two_out[:, columns] = moment_two
        stepped = master - inner_rate * (
            moment_one / (jnp.sqrt(moment_two) + adam_epsilon) + weight_decay * master
        )
        w_out[:, columns] = jnp.where(here, stepped + pseudo - update, stepped)


def finish(frag, keys, *states):
    def spec(array):
        rows, columns = array.shape
        return pl.BlockSpec((rows // FINISH_STEPS, columns), lambda i: (i, 0))

    def like(array):
        return jax.ShapeDtypeStruct(array.shape, array.dtype)

    master = states[2]
    outs = [keys] + [master] * 5
    return pl.pallas_call(
        finish_body,
        grid=(FINISH_STEPS,),
        out_shape=[like(out) for out in outs],
        in_specs=[pl.BlockSpec(memory_space=pltpu.SMEM)] + [spec(a) for a in (keys,) + states],
        out_specs=[spec(out) for out in outs],
        cost_estimate=pl.CostEstimate(flops=30 * master.size, bytes_accessed=26 * master.size, transcendentals=2 * master.size),
    )(frag, keys, *states)


def shards(
    inputs, cotangent, weights, first_moment, second_moment, pseudo_grad, anchor, momentum, fragment
):
    keys, gradient, summed = exchange(inputs[0], cotangent[0], weights[0], pseudo_grad[0])
    keys, *states = finish(
        fragment, keys, gradient, summed, weights[0], first_moment[0], second_moment[0],
        pseudo_grad[0], anchor, momentum,
    )
    return keys[None], states[0][None], states[1][None], states[2][None], states[3], states[4]


def solution(mesh):
    return jax.shard_map(
        shards,
        mesh=mesh,
        in_specs=(
            P("rep", "fsdp", None),
            P("rep", "fsdp", None),
            P("rep", "fsdp", None),
            P("rep", "fsdp", None),
            P("rep", "fsdp", None),
            P("rep", "fsdp", None),
            P("fsdp", None),
            P("fsdp", None),
            P(),
        ),
        out_specs=(
            P("rep", "fsdp", None),
            P("rep", "fsdp", None),
            P("rep", "fsdp", None),
            P("rep", "fsdp", None),
            P("fsdp", None),
            P("fsdp", None),
        ),
        check_vma=False,
    )
```

```python
import jax
import jax.numpy as jnp
from jax import lax
from jax.experimental import pallas as pl
from jax.experimental.pallas import tpu as pltpu
from jax.sharding import PartitionSpec as P

MESH = pl.DeviceIdType.MESH

beta_one = 0.9
beta_two = 0.95
inner_rate = 0.002
weight_decay = 0.1
adam_epsilon = 1e-08
outer_rate = 0.7
outer_momentum = 0.9

RING = 4
TWO = 2
PEERS = 8
COMBOS = RING * TWO
SIDE = 256
HALF = SIDE // 2
COT_PARTS = 3
FINISH_STEPS = 2

OWN, PAIR, FAR, CROSS = range(4)
GATHER_ORDER = (OWN, CROSS, PAIR, FAR)
VIA = (CROSS, PAIR)
BY_Z = (FAR,)
Z_DTYPE = jnp.float32

GATHER_RING = 0
GATHER_CROSS = GATHER_RING + TWO * RING * 2
GATHER_Z = GATHER_CROSS + TWO * RING * 2
TRADE = GATHER_Z + RING * 2
TRADE_COT = TRADE + COMBOS * 2 * 2
REDUCE_CROSS = TRADE_COT + 2 * COT_PARTS
REDUCE_RING = REDUCE_CROSS + COMBOS * 2
REDUCE_Z = REDUCE_RING + TWO * 2 * 3
KEYS = REDUCE_Z + 2
PSUM_ONE = KEYS + 2
PSUM_TWO = PSUM_ONE + PEERS
N_SEMS = PSUM_TWO + PEERS

PLAN = (
    "C1", "C2", "T0", "T1", "T2", "T3", "G1", "G2", "T4", "L0", "W0", "F0", "G3", "F1", "S0", "F2",
    "T5", "S1", "R0", "F3", "S2", "G4", "F4", "F5", "P4", "T6", "S3", "T7", "P5", "G5", "G6", "G7",
    "P3", "F6", "S4", "P6", "S5", "F7", "P7", "P1", "P2", "P0", "K0", "S6", "D0", "S7",
)


def flip(at, where):
    return (at, at + 1 - 2 * (at % 2), (at + 2) % 4, 3 - at)[where]


def body(
    x_hbm, c_hbm, w_hbm, p_hbm, proj_ref, grad_ref, delta_ref,
    xc, cb, ct, wf, wg, acc, acc_pair, keys, keys_in,
    cross, cross_in, around, around_in,
    zs, zr, pg, pr, dl, load_sem, ss, rs,
):
    fsdp = lax.axis_index("fsdp")
    rep = lax.axis_index("rep")
    x, y, z = fsdp // 8, (fsdp // 2) % 4, fsdp % 2
    tokens, width = c_hbm.shape

    def place(h, first, second, zz):
        dx, dy = (first, second) if h == 0 else (second, first)
        return flip(x, dx) * 8 + flip(y, dy) * 2 + zz

    other_z = fsdp + 1 - 2 * z

    def send(src, dst, sem, device, axis="fsdp"):
        return pltpu.make_async_remote_copy(
            src_ref=src, dst_ref=dst, send_sem=ss.at[sem], recv_sem=rs.at[sem],
            device_id={axis: device}, device_id_type=MESH,
        )

    flying = []

    def go(copy):
        copy.start()
        flying.append(copy)

    def settle(keep):
        while len(flying) > keep:
            flying.pop(0).wait_send()

    def reduce_round(c):
        zi, j = divmod(c, RING)
        other = PAIR + CROSS - VIA[zi]
        return zi, j, (z + 1 + zi) % 2, (FAR, VIA[zi], other, OWN)[j]

    load_w = pltpu.make_async_copy(w_hbm, wf, load_sem.at[0])
    load_c = pltpu.make_async_copy(c_hbm, cb.at[0], load_sem.at[1])
    load_p = pltpu.make_async_copy(p_hbm, pg, load_sem.at[2])
    load_w.start()
    load_c.start()
    load_p.start()

    barrier = pltpu.get_barrier_semaphore()
    near = [place(0, PAIR, OWN, z), place(0, CROSS, OWN, z), place(1, PAIR, OWN, z), place(1, CROSS, OWN, z), other_z]
    for device in near:
        pl.semaphore_signal(barrier, inc=1, device_id={"fsdp": device}, device_id_type=MESH)
    for i in range(1, PEERS):
        pl.semaphore_signal(barrier, inc=1, device_id={"rep": (rep + i) % PEERS}, device_id_type=MESH)

    def block(f, h):
        return x_hbm.at[:, pl.ds(pl.multiple_of(f * SIDE + h * HALF, HALF), HALF)]

    def trade_cot(h, part):
        rows = pl.ds(part * HALF, HALF)
        return send(c_hbm.at[rows], cb.at[1 + h, rows], TRADE_COT + h * COT_PARTS + part, place(h, PAIR, OWN, z))

    def cot_start(part):
        for h in range(2):
            go(trade_cot(h, part))

    def cot_wait(_):
        for h in range(2):
            for part in range(COT_PARTS):
                trade_cot(h, part).wait_recv()
            ct[h, :, tokens : 2 * tokens] = narrow(widen(cb[1 + h]).T)

    def trade(c, h, i, who):
        _, _, zz, there = reduce_round(c)
        f = place(h, who, there, zz)
        sem = TRADE + (c * 2 + h) * 2 + i
        return send(block(f, h), xc.at[f, h, pl.ds(tokens, tokens)], sem, place(h, PAIR, OWN, z))

    def trade_start(c):
        for h in range(2):
            go(trade(c, h, 0, FAR))
            go(trade(c, h, 1, PAIR))

    arrived = set()

    def need(c, h, i):
        if (c, h, i) not in arrived:
            trade(c, h, i, (CROSS, OWN)[i]).wait_recv()
            arrived.add((c, h, i))

    def gather_ring(r, h, f, where, to):
        return send(wg.at[f, h], wg.at[f, h], GATHER_RING + (r * RING + where) * 2 + h, place(h, OWN, to, z))

    def gather_cross(r, h, f, where):
        return send(wg.at[f, h], wg.at[f, h], GATHER_CROSS + (r * RING + where) * 2 + h, place(h, CROSS, OWN, z))

    def gather_z(h, f, where):
        return send(wg.at[f, h], wg.at[f, h], GATHER_Z + where * 2 + h, other_z)

    def gather_step(a):
        r, j = divmod(a, RING)
        where = GATHER_ORDER[j]
        for h in range(2):
            f = place(h, OWN, where, (z + r) % 2)
            if r == 1 and (where == OWN or where in BY_Z):
                gather_z(h, f, where).wait_recv()
            elif where != OWN:
                gather_ring(r, h, f, where, PAIR).wait_recv()
            if where == OWN:
                for to in (PAIR, CROSS):
                    if r == 0 or to not in BY_Z:
                        go(gather_ring(r, h, f, to, to))
            elif where == PAIR and (r == 0 or FAR not in BY_Z):
                go(gather_ring(r, h, f, FAR, PAIR + CROSS - where))
            if r == 0 and (where == OWN or where in BY_Z):
                go(gather_z(h, f, where))
            go(gather_cross(r, h, f, where))

    seen = []

    def project(c):
        zi, _, zz, there = reduce_round(c)
        for h in range(2):
            mine, crossed = place(h, OWN, there, zz), place(h, CROSS, there, zz)
            need(c, h, 0)
            need(c, h, 1)
            gather_cross(1 - zi, h, crossed, there).wait_recv()
            value = jnp.dot(xc[mine, h], wg[mine, h], preferred_element_type=jnp.float32)
            value += jnp.dot(xc[crossed, h], wg[crossed, h], preferred_element_type=jnp.float32)
            acc[...] = value[:tokens] + acc[...] if seen else value[:tokens]
            acc_pair[h] = value[tokens:] + acc_pair[h] if len(seen) > 1 else value[tokens:]
            seen.append(c)

    def keys_copy(h):
        return send(keys.at[h], keys_in.at[h], KEYS + h, place(h, PAIR, OWN, z))

    def keys_start(_):
        for h in range(2):
            keys[h] = narrow(acc_pair[h])
            go(keys_copy(h))

    def partial(f, h):
        return jnp.dot(ct[h], xc[f, h], preferred_element_type=jnp.float32)

    def widen(value):
        return value.astype(jnp.float32)

    def narrow(value):
        return value.astype(jnp.bfloat16)

    def reduce_cross(c, h):
        return send(cross.at[c, h], cross_in.at[c, h], REDUCE_CROSS + c * 2 + h, place(h, CROSS, OWN, z))

    def reduce_ring(zi, h, j, to):
        slot = (zi, h, j)
        return send(around.at[slot], around_in.at[slot], REDUCE_RING + (zi * 2 + h) * 3 + j, place(h, OWN, to, z))

    def reduce_z(h):
        return send(zs.at[h], zr.at[h], REDUCE_Z + h, other_z)

    def reduce_first(c):
        _, _, zz, there = reduce_round(c)
        for h in range(2):
            need(c, h, 0)
            cross[c, h] = narrow(partial(place(h, CROSS, there, zz), h))
            go(reduce_cross(c, h))

    def reduce_second(c):
        zi, j, zz, there = reduce_round(c)
        for h in range(2):
            need(c, h, 1)
            value = partial(place(h, OWN, there, zz), h)
            reduce_cross(c, h).wait_recv()
            value = value + widen(cross_in[c, h])
            if j == 2:
                reduce_ring(zi, h, 0, PAIR).wait_recv()
                value = value + widen(around_in[zi, h, 0])
            if j < 3:
                around[zi, h, j] = narrow(value)
                go(reduce_ring(zi, h, j, VIA[zi] if j == 0 else there))
            else:
                for i in (1, 2):
                    reduce_ring(zi, h, i, PAIR).wait_recv()
                    value = value + widen(around_in[zi, h, i])
                if zi == 0:
                    zs[h] = value.astype(Z_DTYPE)
                    go(reduce_z(h))
                else:
                    reduce_z(h).wait_recv()
                    grad_ref[h * HALF : (h + 1) * HALF] = (value + widen(zr[h])).T

    share = SIDE // PEERS

    def share_of(device):
        return pl.ds(pl.multiple_of(device * share, share), share)

    def psum_one(i):
        peer = (rep + i) % PEERS
        return send(pg.at[share_of(peer)], pr.at[rep], PSUM_ONE + i, peer, "rep")

    def psum_two(i):
        peer = (rep + i) % PEERS
        return send(dl.at[share_of(rep)], dl.at[share_of(rep)], PSUM_TWO + i, peer, "rep")

    def psum_turn(_):
        pr[rep] = pg[share_of(rep)]
        for i in range(1, PEERS):
            psum_one(i).wait_recv()
        dl[share_of(rep)] = jnp.sum(pr[...], axis=0)
        for i in range(1, PEERS):
            go(psum_two(i))

    def psum_end(_):
        for i in range(1, PEERS):
            peer = (rep + PEERS - i) % PEERS
            send(dl.at[share_of(peer)], dl.at[share_of(peer)], PSUM_TWO + i, peer, "rep").wait_recv()
        delta_ref[...] = dl[...]
        settle(24)

    pl.semaphore_wait(barrier, len(near) + PEERS - 1)
    cot_start(0)
    load_w.wait()
    for h in range(2):
        wg[fsdp, h] = narrow(wf[h * HALF : (h + 1) * HALF])
    gather_step(0)
    for c in range(COMBOS):
        _, _, zz, there = reduce_round(c)
        for h in range(2):
            for who in (CROSS, OWN):
                f = place(h, who, there, zz)
                pltpu.make_async_copy(block(f, h), xc.at[f, h, pl.ds(0, tokens)], load_sem.at[3]).start()
    load_p.wait()
    for i in range(1, PEERS):
        go(psum_one(i))
    load_c.wait()
    turned = narrow(widen(cb[0]).T)
    ct[0, :, 0:tokens] = turned
    ct[1, :, 0:tokens] = turned
    some = xc.at[pl.ds(0, 16), :, pl.ds(0, tokens)]
    loaded = pltpu.make_async_copy(some, some, load_sem.at[3])

    steps = dict(
        C=cot_start, W=cot_wait, G=gather_step, T=trade_start, P=project, K=keys_start,
        F=reduce_first, S=reduce_second, R=psum_turn, D=psum_end, L=lambda _: loaded.wait(),
    )
    for step in PLAN:
        steps[step[0]](int(step[1]))

    keys_copy(0).wait_recv()
    keys_copy(1).wait_recv()
    proj_ref[...] = narrow(acc[...] + widen(keys_in[0]) + widen(keys_in[1]))

    settle(0)


def exchange(tokens, grads_in, master, pseudo):
    n, depth = tokens.shape
    rows, width = master.shape
    bf16, f32 = jnp.bfloat16, jnp.float32
    tall = (width, HALF)
    flops = 4 * n * depth * width
    return pl.pallas_call(
        body,
        out_shape=[
            jax.ShapeDtypeStruct((n, width), bf16),
            jax.ShapeDtypeStruct((rows, width), f32),
            jax.ShapeDtypeStruct(pseudo.shape, f32),
        ],
        in_specs=[pl.BlockSpec(memory_space=pl.ANY)] * 4,
        out_specs=[pl.BlockSpec(memory_space=pltpu.VMEM)] * 3,
        scratch_shapes=[
            pltpu.VMEM((32, 2, 2 * n, HALF), bf16),
            pltpu.VMEM((3, n, width), bf16),
            pltpu.VMEM((2, width, 2 * n), bf16),
            pltpu.VMEM((rows, width), f32),
            pltpu.VMEM((32, 2, HALF, width), bf16),
            pltpu.VMEM((n, width), f32),
            pltpu.VMEM((2, n, width), f32),
            pltpu.VMEM((2, n, width), bf16),
            pltpu.VMEM((2, n, width), bf16),
            pltpu.VMEM((COMBOS, 2) + tall, bf16),
            pltpu.VMEM((COMBOS, 2) + tall, bf16),
            pltpu.VMEM((TWO, 2, 3) + tall, bf16),
            pltpu.VMEM((TWO, 2, 3) + tall, bf16),
            pltpu.VMEM((2,) + tall, Z_DTYPE),
            pltpu.VMEM((2,) + tall, Z_DTYPE),
            pltpu.VMEM(pseudo.shape, f32),
            pltpu.VMEM((PEERS, SIDE // PEERS, pseudo.shape[1]), f32),
            pltpu.VMEM(pseudo.shape, f32),
            pltpu.SemaphoreType.DMA((4,)),
            pltpu.SemaphoreType.DMA((N_SEMS,)),
            pltpu.SemaphoreType.DMA((N_SEMS,)),
        ],
        compiler_params=pltpu.CompilerParams(
            collective_id=0, has_side_effects=True, vmem_limit_bytes=58 * 2**20
        ),
        cost_estimate=pl.CostEstimate(flops=flops, bytes_accessed=12 * 2**20, transcendentals=0),
    )(tokens, grads_in, master, pseudo)


def finish_body(
    frag_ref, keys_ref, grad_ref, delta_ref, w_ref, one_ref, two_ref, pseudo_ref, anchor_ref, mom_ref,
    keys_out, w_out, one_out, two_out, anchor_out, mom_out,
):
    frag = frag_ref[0]
    keys_out[...] = keys_ref[...]
    frag_w = delta_ref.shape[1]
    mean_delta = delta_ref[...] / PEERS
    pseudo = pseudo_ref[...]
    for q in range(w_ref.shape[1] // frag_w):
        columns = slice(q * frag_w, (q + 1) * frag_w)
        here = frag == q
        momentum, anchor = mom_ref[:, columns], anchor_ref[:, columns]
        new_momentum = outer_momentum * momentum + mean_delta
        update = outer_rate * (outer_momentum * new_momentum + mean_delta)
        mom_out[:, columns] = jnp.where(here, new_momentum, momentum)
        anchor_out[:, columns] = jnp.where(here, anchor - update, anchor)
        master, gradient = w_ref[:, columns], grad_ref[:, columns]
        moment_one = beta_one * one_ref[:, columns] + (1.0 - beta_one) * gradient
        moment_two = beta_two * two_ref[:, columns] + (1.0 - beta_two) * gradient * gradient
        one_out[:, columns] = moment_one
        two_out[:, columns] = moment_two
        stepped = master - inner_rate * (
            moment_one / (jnp.sqrt(moment_two) + adam_epsilon) + weight_decay * master
        )
        w_out[:, columns] = jnp.where(here, stepped + pseudo - update, stepped)


def finish(frag, keys, *states):
    def spec(array):
        rows, columns = array.shape
        return pl.BlockSpec((rows // FINISH_STEPS, columns), lambda i: (i, 0))

    def like(array):
        return jax.ShapeDtypeStruct(array.shape, array.dtype)

    master = states[2]
    outs = [keys] + [master] * 5
    return pl.pallas_call(
        finish_body,
        grid=(FINISH_STEPS,),
        out_shape=[like(out) for out in outs],
        in_specs=[pl.BlockSpec(memory_space=pltpu.SMEM)] + [spec(a) for a in (keys,) + states],
        out_specs=[spec(out) for out in outs],
        cost_estimate=pl.CostEstimate(flops=30 * master.size, bytes_accessed=26 * master.size, transcendentals=2 * master.size),
    )(frag, keys, *states)


def shards(
    inputs, cotangent, weights, first_moment, second_moment, pseudo_grad, anchor, momentum, fragment
):
    keys, gradient, summed = exchange(inputs[0], cotangent[0], weights[0], pseudo_grad[0])
    keys, *states = finish(
        fragment, keys, gradient, summed, weights[0], first_moment[0], second_moment[0],
        pseudo_grad[0], anchor, momentum,
    )
    return keys[None], states[0][None], states[1][None], states[2][None], states[3], states[4]


def solution(mesh):
    return jax.shard_map(
        shards,
        mesh=mesh,
        in_specs=(
            P("rep", "fsdp", None),
            P("rep", "fsdp", None),
            P("rep", "fsdp", None),
            P("rep", "fsdp", None),
            P("rep", "fsdp", None),
            P("rep", "fsdp", None),
            P("fsdp", None),
            P("fsdp", None),
            P(),
        ),
        out_specs=(
            P("rep", "fsdp", None),
            P("rep", "fsdp", None),
            P("rep", "fsdp", None),
            P("rep", "fsdp", None),
            P("fsdp", None),
            P("fsdp", None),
        ),
        check_vma=False,
    )
```

```python
import jax
import jax.numpy as jnp
from jax import lax
from jax.experimental import pallas as pl
from jax.experimental.pallas import tpu as pltpu
from jax.sharding import PartitionSpec as P

MESH = pl.DeviceIdType.MESH

beta_one = 0.9
beta_two = 0.95
inner_rate = 0.002
weight_decay = 0.1
adam_epsilon = 1e-08
outer_rate = 0.7
outer_momentum = 0.9

RING = 4
TWO = 2
PEERS = 8
COMBOS = RING * TWO
SIDE = 256
HALF = SIDE // 2
COT_PARTS = 3
FINISH_STEPS = 2

OWN, PAIR, FAR, CROSS = range(4)
GATHER_ORDER = (OWN, CROSS, PAIR, FAR)
VIA = (CROSS, PAIR)
BY_Z = (FAR,)
Z_DTYPE = jnp.float32

GATHER_RING = 0
GATHER_CROSS = GATHER_RING + TWO * RING * 2
GATHER_Z = GATHER_CROSS + TWO * RING * 2
TRADE = GATHER_Z + RING * 2
TRADE_COT = TRADE + COMBOS * 2 * 2
REDUCE_CROSS = TRADE_COT + 2 * COT_PARTS
REDUCE_RING = REDUCE_CROSS + COMBOS * 2
REDUCE_Z = REDUCE_RING + TWO * 2 * 3
KEYS = REDUCE_Z + 2
PSUM_ONE = KEYS + 2
PSUM_TWO = PSUM_ONE + PEERS
N_SEMS = PSUM_TWO + PEERS

PLAN = (
    "C1", "C2", "T0", "T1", "T2", "T3", "G1", "G2", "T4", "L0", "W0", "F0", "G3", "F1", "S0", "R0", "F2",
    "T5", "S1", "F3", "S2", "G4", "F4", "F5", "P4", "T6", "S3", "T7", "P5", "G5", "G6", "G7",
    "P3", "F6", "S4", "P6", "S5", "F7", "P7", "P1", "P2", "P0", "K0", "S6", "D0", "S7",
)


def flip(at, where):
    return (at, at + 1 - 2 * (at % 2), (at + 2) % 4, 3 - at)[where]


def body(
    x_hbm, c_hbm, w_hbm, p_hbm, proj_ref, grad_ref, delta_ref,
    xc, cb, ct, wf, wg, acc, acc_pair, keys, keys_in,
    cross, cross_in, around, around_in,
    zs, zr, pg, pr, dl, load_sem, ss, rs,
):
    fsdp = lax.axis_index("fsdp")
    rep = lax.axis_index("rep")
    x, y, z = fsdp // 8, (fsdp // 2) % 4, fsdp % 2
    tokens, width = c_hbm.shape

    def place(h, first, second, zz):
        dx, dy = (first, second) if h == 0 else (second, first)
        return flip(x, dx) * 8 + flip(y, dy) * 2 + zz

    other_z = fsdp + 1 - 2 * z

    def send(src, dst, sem, device, axis="fsdp"):
        return pltpu.make_async_remote_copy(
            src_ref=src, dst_ref=dst, send_sem=ss.at[sem], recv_sem=rs.at[sem],
            device_id={axis: device}, device_id_type=MESH,
        )

    flying = []

    def go(copy):
        copy.start()
        flying.append(copy)

    def settle(keep):
        while len(flying) > keep:
            flying.pop(0).wait_send()

    def reduce_round(c):
        zi, j = divmod(c, RING)
        other = PAIR + CROSS - VIA[zi]
        return zi, j, (z + 1 + zi) % 2, (FAR, VIA[zi], other, OWN)[j]

    load_w = pltpu.make_async_copy(w_hbm, wf, load_sem.at[0])
    load_c = pltpu.make_async_copy(c_hbm, cb.at[0], load_sem.at[1])
    load_p = pltpu.make_async_copy(p_hbm, pg, load_sem.at[2])
    load_w.start()
    load_c.start()
    load_p.start()

    barrier = pltpu.get_barrier_semaphore()
    near = [place(0, PAIR, OWN, z), place(0, CROSS, OWN, z), place(1, PAIR, OWN, z), place(1, CROSS, OWN, z), other_z]
    for device in near:
        pl.semaphore_signal(barrier, inc=1, device_id={"fsdp": device}, device_id_type=MESH)
    for i in range(1, PEERS):
        pl.semaphore_signal(barrier, inc=1, device_id={"rep": (rep + i) % PEERS}, device_id_type=MESH)

    def block(f, h):
        return x_hbm.at[:, pl.ds(pl.multiple_of(f * SIDE + h * HALF, HALF), HALF)]

    def trade_cot(h, part):
        rows = pl.ds(part * HALF, HALF)
        return send(c_hbm.at[rows], cb.at[1 + h, rows], TRADE_COT + h * COT_PARTS + part, place(h, PAIR, OWN, z))

    def cot_start(part):
        for h in range(2):
            go(trade_cot(h, part))

    def cot_wait(_):
        for h in range(2):
            for part in range(COT_PARTS):
                trade_cot(h, part).wait_recv()
            ct[h, :, tokens : 2 * tokens] = narrow(widen(cb[1 + h]).T)

    def trade(c, h, i, who):
        _, _, zz, there = reduce_round(c)
        f = place(h, who, there, zz)
        sem = TRADE + (c * 2 + h) * 2 + i
        return send(block(f, h), xc.at[f, h, pl.ds(tokens, tokens)], sem, place(h, PAIR, OWN, z))

    def trade_start(c):
        for h in range(2):
            go(trade(c, h, 0, FAR))
            go(trade(c, h, 1, PAIR))

    arrived = set()

    def need(c, h, i):
        if (c, h, i) not in arrived:
            trade(c, h, i, (CROSS, OWN)[i]).wait_recv()
            arrived.add((c, h, i))

    def gather_ring(r, h, f, where, to):
        return send(wg.at[f, h], wg.at[f, h], GATHER_RING + (r * RING + where) * 2 + h, place(h, OWN, to, z))

    def gather_cross(r, h, f, where):
        return send(wg.at[f, h], wg.at[f, h], GATHER_CROSS + (r * RING + where) * 2 + h, place(h, CROSS, OWN, z))

    def gather_z(h, f, where):
        return send(wg.at[f, h], wg.at[f, h], GATHER_Z + where * 2 + h, other_z)

    def gather_step(a):
        r, j = divmod(a, RING)
        where = GATHER_ORDER[j]
        for h in range(2):
            f = place(h, OWN, where, (z + r) % 2)
            if r == 1 and (where == OWN or where in BY_Z):
                gather_z(h, f, where).wait_recv()
            elif where != OWN:
                gather_ring(r, h, f, where, PAIR).wait_recv()
            if where == OWN:
                for to in (PAIR, CROSS):
                    if r == 0 or to not in BY_Z:
                        go(gather_ring(r, h, f, to, to))
            elif where == PAIR and (r == 0 or FAR not in BY_Z):
                go(gather_ring(r, h, f, FAR, PAIR + CROSS - where))
            if r == 0 and (where == OWN or where in BY_Z):
                go(gather_z(h, f, where))
            go(gather_cross(r, h, f, where))

    seen = []

    def project(c):
        zi, _, zz, there = reduce_round(c)
        for h in range(2):
            mine, crossed = place(h, OWN, there, zz), place(h, CROSS, there, zz)
            need(c, h, 0)
            need(c, h, 1)
            gather_cross(1 - zi, h, crossed, there).wait_recv()
            value = jnp.dot(xc[mine, h], wg[mine, h], preferred_element_type=jnp.float32)
            value += jnp.dot(xc[crossed, h], wg[crossed, h], preferred_element_type=jnp.float32)
            acc[...] = value[:tokens] + acc[...] if seen else value[:tokens]
            acc_pair[h] = value[tokens:] + acc_pair[h] if len(seen) > 1 else value[tokens:]
            seen.append(c)

    def keys_copy(h):
        return send(keys.at[h], keys_in.at[h], KEYS + h, place(h, PAIR, OWN, z))

    def keys_start(_):
        for h in range(2):
            keys[h] = narrow(acc_pair[h])
            go(keys_copy(h))

    def partial(f, h):
        return jnp.dot(ct[h], xc[f, h], preferred_element_type=jnp.float32)

    def widen(value):
        return value.astype(jnp.float32)

    def narrow(value):
        return value.astype(jnp.bfloat16)

    def reduce_cross(c, h):
        return send(cross.at[c, h], cross_in.at[c, h], REDUCE_CROSS + c * 2 + h, place(h, CROSS, OWN, z))

    def reduce_ring(zi, h, j, to):
        slot = (zi, h, j)
        return send(around.at[slot], around_in.at[slot], REDUCE_RING + (zi * 2 + h) * 3 + j, place(h, OWN, to, z))

    def reduce_z(h):
        return send(zs.at[h], zr.at[h], REDUCE_Z + h, other_z)

    def reduce_first(c):
        _, _, zz, there = reduce_round(c)
        for h in range(2):
            need(c, h, 0)
            cross[c, h] = narrow(partial(place(h, CROSS, there, zz), h))
            go(reduce_cross(c, h))

    def reduce_second(c):
        zi, j, zz, there = reduce_round(c)
        for h in range(2):
            need(c, h, 1)
            value = partial(place(h, OWN, there, zz), h)
            reduce_cross(c, h).wait_recv()
            value = value + widen(cross_in[c, h])
            if j == 2:
                reduce_ring(zi, h, 0, PAIR).wait_recv()
                value = value + widen(around_in[zi, h, 0])
            if j < 3:
                around[zi, h, j] = narrow(value)
                go(reduce_ring(zi, h, j, VIA[zi] if j == 0 else there))
            else:
                for i in (1, 2):
                    reduce_ring(zi, h, i, PAIR).wait_recv()
                    value = value + widen(around_in[zi, h, i])
                if zi == 0:
                    zs[h] = value.astype(Z_DTYPE)
                    go(reduce_z(h))
                else:
                    reduce_z(h).wait_recv()
                    grad_ref[h * HALF : (h + 1) * HALF] = (value + widen(zr[h])).T

    share = SIDE // PEERS

    def share_of(device):
        return pl.ds(pl.multiple_of(device * share, share), share)

    def psum_one(i):
        peer = (rep + i) % PEERS
        return send(pg.at[share_of(peer)], pr.at[rep], PSUM_ONE + i, peer, "rep")

    def psum_two(i):
        peer = (rep + i) % PEERS
        return send(dl.at[share_of(rep)], dl.at[share_of(rep)], PSUM_TWO + i, peer, "rep")

    def psum_turn(_):
        pr[rep] = pg[share_of(rep)]
        for i in range(1, PEERS):
            psum_one(i).wait_recv()
        dl[share_of(rep)] = jnp.sum(pr[...], axis=0)
        for i in range(1, PEERS):
            go(psum_two(i))

    def psum_end(_):
        for i in range(1, PEERS):
            peer = (rep + PEERS - i) % PEERS
            send(dl.at[share_of(peer)], dl.at[share_of(peer)], PSUM_TWO + i, peer, "rep").wait_recv()
        delta_ref[...] = dl[...]
        settle(24)

    pl.semaphore_wait(barrier, len(near) + PEERS - 1)
    cot_start(0)
    load_w.wait()
    for h in range(2):
        wg[fsdp, h] = narrow(wf[h * HALF : (h + 1) * HALF])
    gather_step(0)
    for c in range(COMBOS):
        _, _, zz, there = reduce_round(c)
        for h in range(2):
            for who in (CROSS, OWN):
                f = place(h, who, there, zz)
                pltpu.make_async_copy(block(f, h), xc.at[f, h, pl.ds(0, tokens)], load_sem.at[3]).start()
    load_p.wait()
    for i in range(1, PEERS):
        go(psum_one(i))
    load_c.wait()
    turned = narrow(widen(cb[0]).T)
    ct[0, :, 0:tokens] = turned
    ct[1, :, 0:tokens] = turned
    some = xc.at[pl.ds(0, 16), :, pl.ds(0, tokens)]
    loaded = pltpu.make_async_copy(some, some, load_sem.at[3])

    steps = dict(
        C=cot_start, W=cot_wait, G=gather_step, T=trade_start, P=project, K=keys_start,
        F=reduce_first, S=reduce_second, R=psum_turn, D=psum_end, L=lambda _: loaded.wait(),
    )
    for step in PLAN:
        steps[step[0]](int(step[1]))

    keys_copy(0).wait_recv()
    keys_copy(1).wait_recv()
    proj_ref[...] = narrow(acc[...] + widen(keys_in[0]) + widen(keys_in[1]))

    settle(0)


def exchange(tokens, grads_in, master, pseudo):
    n, depth = tokens.shape
    rows, width = master.shape
    bf16, f32 = jnp.bfloat16, jnp.float32
    tall = (width, HALF)
    flops = 4 * n * depth * width
    return pl.pallas_call(
        body,
        out_shape=[
            jax.ShapeDtypeStruct((n, width), bf16),
            jax.ShapeDtypeStruct((rows, width), f32),
            jax.ShapeDtypeStruct(pseudo.shape, f32),
        ],
        in_specs=[pl.BlockSpec(memory_space=pl.ANY)] * 4,
        out_specs=[pl.BlockSpec(memory_space=pltpu.VMEM)] * 3,
        scratch_shapes=[
            pltpu.VMEM((32, 2, 2 * n, HALF), bf16),
            pltpu.VMEM((3, n, width), bf16),
            pltpu.VMEM((2, width, 2 * n), bf16),
            pltpu.VMEM((rows, width), f32),
            pltpu.VMEM((32, 2, HALF, width), bf16),
            pltpu.VMEM((n, width), f32),
            pltpu.VMEM((2, n, width), f32),
            pltpu.VMEM((2, n, width), bf16),
            pltpu.VMEM((2, n, width), bf16),
            pltpu.VMEM((COMBOS, 2) + tall, bf16),
            pltpu.VMEM((COMBOS, 2) + tall, bf16),
            pltpu.VMEM((TWO, 2, 3) + tall, bf16),
            pltpu.VMEM((TWO, 2, 3) + tall, bf16),
            pltpu.VMEM((2,) + tall, Z_DTYPE),
            pltpu.VMEM((2,) + tall, Z_DTYPE),
            pltpu.VMEM(pseudo.shape, f32),
            pltpu.VMEM((PEERS, SIDE // PEERS, pseudo.shape[1]), f32),
            pltpu.VMEM(pseudo.shape, f32),
            pltpu.SemaphoreType.DMA((4,)),
            pltpu.SemaphoreType.DMA((N_SEMS,)),
            pltpu.SemaphoreType.DMA((N_SEMS,)),
        ],
        compiler_params=pltpu.CompilerParams(
            collective_id=0, has_side_effects=True, vmem_limit_bytes=58 * 2**20
        ),
        cost_estimate=pl.CostEstimate(flops=flops, bytes_accessed=12 * 2**20, transcendentals=0),
    )(tokens, grads_in, master, pseudo)


def finish_body(
    frag_ref, keys_ref, grad_ref, delta_ref, w_ref, one_ref, two_ref, pseudo_ref, anchor_ref, mom_ref,
    keys_out, w_out, one_out, two_out, anchor_out, mom_out,
):
    frag = frag_ref[0]
    keys_out[...] = keys_ref[...]
    frag_w = delta_ref.shape[1]
    mean_delta = delta_ref[...] / PEERS
    pseudo = pseudo_ref[...]
    for q in range(w_ref.shape[1] // frag_w):
        columns = slice(q * frag_w, (q + 1) * frag_w)
        here = frag == q
        momentum, anchor = mom_ref[:, columns], anchor_ref[:, columns]
        new_momentum = outer_momentum * momentum + mean_delta
        update = outer_rate * (outer_momentum * new_momentum + mean_delta)
        mom_out[:, columns] = jnp.where(here, new_momentum, momentum)
        anchor_out[:, columns] = jnp.where(here, anchor - update, anchor)
        master, gradient = w_ref[:, columns], grad_ref[:, columns]
        moment_one = beta_one * one_ref[:, columns] + (1.0 - beta_one) * gradient
        moment_two = beta_two * two_ref[:, columns] + (1.0 - beta_two) * gradient * gradient
        one_out[:, columns] = moment_one
        two_out[:, columns] = moment_two
        stepped = master - inner_rate * (
            moment_one / (jnp.sqrt(moment_two) + adam_epsilon) + weight_decay * master
        )
        w_out[:, columns] = jnp.where(here, stepped + pseudo - update, stepped)


def finish(frag, keys, *states):
    def spec(array):
        rows, columns = array.shape
        return pl.BlockSpec((rows // FINISH_STEPS, columns), lambda i: (i, 0))

    def like(array):
        return jax.ShapeDtypeStruct(array.shape, array.dtype)

    master = states[2]
    outs = [keys] + [master] * 5
    return pl.pallas_call(
        finish_body,
        grid=(FINISH_STEPS,),
        out_shape=[like(out) for out in outs],
        in_specs=[pl.BlockSpec(memory_space=pltpu.SMEM)] + [spec(a) for a in (keys,) + states],
        out_specs=[spec(out) for out in outs],
        cost_estimate=pl.CostEstimate(flops=30 * master.size, bytes_accessed=26 * master.size, transcendentals=2 * master.size),
    )(frag, keys, *states)


def shards(
    inputs, cotangent, weights, first_moment, second_moment, pseudo_grad, anchor, momentum, fragment
):
    keys, gradient, summed = exchange(inputs[0], cotangent[0], weights[0], pseudo_grad[0])
    keys, *states = finish(
        fragment, keys, gradient, summed, weights[0], first_moment[0], second_moment[0],
        pseudo_grad[0], anchor, momentum,
    )
    return keys[None], states[0][None], states[1][None], states[2][None], states[3], states[4]


def solution(mesh):
    return jax.shard_map(
        shards,
        mesh=mesh,
        in_specs=(
            P("rep", "fsdp", None),
            P("rep", "fsdp", None),
            P("rep", "fsdp", None),
            P("rep", "fsdp", None),
            P("rep", "fsdp", None),
            P("rep", "fsdp", None),
            P("fsdp", None),
            P("fsdp", None),
            P(),
        ),
        out_specs=(
            P("rep", "fsdp", None),
            P("rep", "fsdp", None),
            P("rep", "fsdp", None),
            P("rep", "fsdp", None),
            P("fsdp", None),
            P("fsdp", None),
        ),
        check_vma=False,
    )
```
